32 devices in a mesh: ha: 16 (over z, y, x), ta: 2 (over core).
Axes of the slice: x: 2, y: 2, z: 4, core: 2. Of those that a mesh axis runs over, the one named last changes fastest.
Arguments:
- features: bfloat16 [8, 16, 640, 128], P('ta', 'ha'), may hold values from -6 to 6
- cotangent: bfloat16 [8, 16, 640, 128], P('ta', 'ha'), may hold values from -6 to 6
- kernel: bfloat16 [3, 3, 3, 128, 128], replicated, may hold values from -0.109375 to 0.109375
Outputs:
- grad_features: bfloat16 [8, 16, 640, 128], P('ta', 'ha')
- grad_kernel: float32 [3456, 128], P(('ha', 'ta'))
The draws below stay inside these ranges and needn't reach their ends.
All inputs are finite; a program needn't handle non-finite values.
Results may differ from the reference program's by a relative error of at most 0.003.
Values may be sent and summed in bfloat16 or wider, within the bound.
A program may use at most 128 MiB of HBM per device.

```python
import jax
import jax.numpy as jnp
from jax import lax

C = 128
TAPS = 27
WIDTH = 640
FRAMES = 8
HEIGHT = 16


def block_scale(stream_key, dims, shards, smallest, largest):
    level, own = 1.0, jax.random.fold_in(stream_key, 6)
    for position, blocks in shards:
        heights = jnp.exp(jax.random.uniform(jax.random.fold_in(own, position), (blocks,), jnp.float32, smallest / len(shards), largest / len(shards)))
        level = level * jnp.repeat(heights, dims[position] // blocks).reshape([-1 if axis == position else 1 for axis in range(len(dims))])
    return level


def normal_values(stream_key, extent, deviation, most, pieces=(), kind=jnp.bfloat16):
    result = jax.random.normal(stream_key, extent, jnp.float32) * deviation
    if len(pieces) > 0:
        result = block_scale(stream_key, extent, pieces, -0.22, 0.18) * result
    return jnp.clip(result, min=-most, max=most).astype(kind)


def setup_inputs(seed: int = 0) -> dict:
    arg_keys = jax.random.split(jax.random.key(seed), 4)
    return {
        "features": normal_values(arg_keys[0], (FRAMES, HEIGHT, WIDTH, C), 1.0, 6.0, ((0, 2), (1, 16))),
        "cotangent": normal_values(arg_keys[1], (FRAMES, HEIGHT, WIDTH, C), 1.0, 6.0, ((0, 2), (1, 16))),
        "kernel": normal_values(arg_keys[2], (3, 3, 3, C, C), (TAPS * C) ** -0.5, 0.109375),
    }


def reference(features, cotangent, kernel):
    frames, height, breadth, channels = features.shape
    values = features.astype(jnp.float32)
    active = jax.nn.silu(values).astype(jnp.bfloat16)
    act_pad = jnp.pad(active, ((2, 0), (1, 1), (1, 1), (0, 0)))
    cot_pad = jnp.pad(cotangent, ((0, 2), (1, 1), (1, 1), (0, 0)))
    cot_flat = cotangent.reshape(-1, channels)
    grad_input = jnp.zeros((frames * height * breadth, channels), jnp.float32)
    blocks = []
    for t_tap in range(3):
        for h_tap in range(3):
            cot_slab = jnp.concatenate([cot_pad[2 - t_tap:2 - t_tap + frames, 2 - h_tap:2 - h_tap + height, 2 - w_tap:2 - w_tap + breadth] for w_tap in range(3)], axis=-1).reshape(-1, 3 * channels)
            stacked = jnp.transpose(kernel[t_tap, h_tap], (0, 2, 1)).reshape(3 * channels, channels)
            grad_input = grad_input + jnp.dot(cot_slab, stacked, preferred_element_type=jnp.float32)
            act_slab = jnp.concatenate([act_pad[t_tap:t_tap + frames, h_tap:h_tap + height, w_tap:w_tap + breadth] for w_tap in range(3)], axis=-1).reshape(-1, 3 * channels)
            blocks.append(lax.dot_general(act_slab, cot_flat, (((0,), (0,)), ((), ())), preferred_element_type=jnp.float32))
    factor = float(frames * height * breadth) ** -0.5
    grad_kernel = jnp.concatenate(blocks, axis=0) * factor
    sigmoid_part = jax.nn.sigmoid(values)
    derivative = sigmoid_part * (1.0 + values * (1.0 - sigmoid_part))
    grad_features = (cotangent.astype(jnp.float32) + derivative * grad_input.reshape(features.shape)).astype(jnp.bfloat16)
    return grad_features, grad_kernel
```

```python
import jax
import jax.numpy as jnp
from jax import lax
from jax.sharding import PartitionSpec as P


def passed_along(block, axis, distance):
    devices = range(lax.axis_size(axis))
    route = [(i - distance, i) for i in devices if i - distance in devices]
    return lax.ppermute(block, axis, route)


def halo_rows(x, axis):
    count = lax.axis_size(axis)
    up = [(i, i + 1) for i in range(count - 1)]
    down = [(j, i) for i, j in up]
    return lax.ppermute(x, axis, up), lax.ppermute(x, axis, down)


def body(features, cotangent, kernel):
    frames, height, breadth, channels = features.shape
    values = features.astype(jnp.float32)
    active = jax.nn.silu(values).astype(jnp.bfloat16)
    act_flat = active.reshape(-1, channels)
    before, after = halo_rows(cotangent[:, -1:], "ha") if height == 1 else (
        lax.ppermute(cotangent[:, -1:], "ha", [(i, i + 1) for i in range(lax.axis_size("ha") - 1)]),
        lax.ppermute(cotangent[:, :1], "ha", [(i + 1, i) for i in range(lax.axis_size("ha") - 1)]),
    )
    cot_rows = jnp.concatenate([before, cotangent, after], axis=1)
    future = passed_along(cot_rows[:2], "ta", -1)
    cot_ext = jnp.concatenate([cot_rows, future], axis=0)
    cot_pad = jnp.pad(cot_ext, ((0, 0), (0, 0), (1, 1), (0, 0)))
    grad_input = jnp.zeros((frames * height * breadth, channels), jnp.float32)
    blocks = []
    for t_tap in range(3):
        for h_tap in range(3):
            cot_slab = jnp.concatenate(
                [
                    cot_pad[
                        2 - t_tap : 2 - t_tap + frames,
                        2 - h_tap : 2 - h_tap + height,
                        2 - w_tap : 2 - w_tap + breadth,
                    ]
                    for w_tap in range(3)
                ],
                axis=-1,
            ).reshape(-1, 3 * channels)
            stacked = jnp.transpose(kernel[t_tap, h_tap], (0, 2, 1)).reshape(3 * channels, channels)
            grad_input = grad_input + jnp.dot(cot_slab, stacked, preferred_element_type=jnp.float32)
            part = lax.dot_general(
                act_flat, cot_slab, (((0,), (0,)), ((), ())), preferred_element_type=jnp.float32
            )
            blocks += [part[:, k * channels : (k + 1) * channels] for k in range(3)]
    rows, cores = lax.axis_size("ha"), lax.axis_size("ta")
    total_cells = frames * height * breadth * rows * cores
    factor = float(total_cells) ** (-0.5)
    term = (jnp.concatenate(blocks, axis=0) * factor).reshape(rows, cores, -1, channels)
    mine = lax.axis_index("ta")
    kept = lax.dynamic_index_in_dim(term, mine, 1, keepdims=False)
    given = lax.dynamic_index_in_dim(term, 1 - mine, 1, keepdims=False)
    kept = kept + lax.ppermute(given, "ta", [(0, 1), (1, 0)])
    got = lax.all_to_all(kept.astype(jnp.bfloat16), "ha", 0, 0, tiled=True)
    grad_kernel = jnp.sum(got.astype(jnp.float32), axis=0)
    sigmoid_part = jax.nn.sigmoid(values)
    derivative = sigmoid_part * (1.0 + values * (1.0 - sigmoid_part))
    grad_features = (
        cotangent.astype(jnp.float32) + derivative * grad_input.reshape(features.shape)
    ).astype(jnp.bfloat16)
    return (grad_features, grad_kernel)


def solution(mesh):
    placed = (P("ta", "ha", None, None), P("ta", "ha", None, None), P())
    return jax.shard_map(
        body,
        mesh=mesh,
        in_specs=placed,
        out_specs=(P("ta", "ha", None, None), P(("ha", "ta"), None)),
        check_vma=False,
    )
```

```python
import functools

import jax
import jax.numpy as jnp
from jax import lax
from jax.experimental import pallas as pl
from jax.experimental.pallas import tpu as pltpu
from jax.sharding import PartitionSpec as P

MESH = pl.DeviceIdType.MESH
LEAD = 8
CHUNKS = 4


def fused(
    rows, cores, factor,
    feat, cot, kern, grad_features, grad_kernel,
    ext, future, acts, padded, partial, acc, give, got, out, landed,
    halo_send, halo_recv, future_send, future_recv, pass_send, pass_recv,
    pair_send, pair_recv, spread_send, spread_recv,
):
    frames, breadth, channels = feat.shape
    wide = 3 * channels
    share, tall = grad_kernel.shape[0], give.shape[1]
    ha, ta = lax.axis_index("ha"), lax.axis_index("ta")
    mate = 1 - ta

    barrier = pltpu.get_barrier_semaphore()

    def greet(s, _):
        pl.semaphore_signal(barrier, inc=1, device_id=(lax.rem(ha + s, rows), ta), device_id_type=MESH)
        return 0

    lax.fori_loop(1, rows, greet, 0)
    pl.semaphore_signal(barrier, inc=1, device_id=(ha, mate), device_id_type=MESH)
    pl.semaphore_wait(barrier, rows)

    def halo(side, frame):
        return pltpu.make_async_remote_copy(
            src_ref=cot.at[frame],
            dst_ref=ext.at[side, frame],
            send_sem=halo_send.at[side, frame],
            recv_sem=halo_recv.at[side, frame],
            device_id=(ha + 1 if side == 0 else ha - 1, ta),
            device_id_type=MESH,
        )

    def ahead(frame):
        return pltpu.make_async_remote_copy(
            src_ref=cot.at[frame],
            dst_ref=future.at[frame],
            send_sem=future_send.at[frame],
            recv_sem=future_recv.at[frame],
            device_id=(ha, mate),
            device_id_type=MESH,
        )

    def relay(side, frame):
        return pltpu.make_async_remote_copy(
            src_ref=ext.at[side, frame],
            dst_ref=ext.at[side, frames + frame],
            send_sem=pass_send.at[side, frame],
            recv_sem=pass_recv.at[side, frame],
            device_id=(ha, mate),
            device_id_type=MESH,
        )

    sends = (ha < rows - 1, ha > 0)
    takes = (ha > 0, ha < rows - 1)

    for frame in range(frames):
        for side in range(2):
            @pl.when(sends[side])
            def _():
                halo(side, frame).start()

    @pl.when(ta == 1)
    def _():
        for frame in range(2):
            ahead(frame).start()

    for side in range(2):
        @pl.when(jnp.logical_not(takes[side]))
        def _():
            ext[side, :frames] = jnp.zeros((frames, breadth, channels), ext.dtype)

    edge = jnp.zeros((LEAD, channels), jnp.float32)
    padded[:LEAD] = edge
    padded[LEAD + breadth :] = edge
    acc[...] = jnp.zeros_like(acc)

    def activate(t, _):
        v = feat[t].astype(jnp.float32)
        active = v / (1.0 + jnp.exp(-v))
        padded[LEAD : LEAD + breadth] = active
        for k in range(3):
            acts[t, :, k * channels : (k + 1) * channels] = padded[
                LEAD - 1 + k : LEAD - 1 + k + breadth
            ].astype(jnp.bfloat16)
        partial[t] = jnp.zeros(partial.shape[1:], jnp.float32)
        return 0

    lax.fori_loop(0, frames, activate, 0)

    nt = (((1,), (1,)), ((), ()))
    tn = (((0,), (0,)), ((), ()))

    def span(e):
        return max(0, e - 2), min(frames, e + 1)

    def middle(e, source):
        def step(t, _):
            i = t - e + 2
            block = source[...]
            tap = i * 3 + 1
            partial[t, LEAD : LEAD + breadth] += lax.dot_general(
                block, kern[tap], nt, preferred_element_type=jnp.float32
            )
            start = pl.multiple_of(tap * wide, wide)
            acc[pl.ds(start, wide)] += lax.dot_general(
                acts[t], block, tn, preferred_element_type=jnp.float32
            )
            return 0

        lax.fori_loop(*span(e), step, 0)

    def outer(e):
        def step(t, _):
            i = t - e + 2
            block = jnp.concatenate([ext[0, e], ext[1, e]], axis=1)
            weights = jnp.concatenate([kern[i * 3 + 2], kern[i * 3]], axis=1)
            partial[t, LEAD : LEAD + breadth] += lax.dot_general(
                block, weights, nt, preferred_element_type=jnp.float32
            )
            both = lax.dot_general(acts[t], block, tn, preferred_element_type=jnp.float32)
            low = pl.multiple_of((i * 3 + 2) * wide, wide)
            high = pl.multiple_of(i * 3 * wide, wide)
            acc[pl.ds(low, wide)] += both[:, :channels]
            acc[pl.ds(high, wide)] += both[:, channels:]
            return 0

        lax.fori_loop(*span(e), step, 0)

    for e in range(frames):
        middle(e, cot.at[e])

    @pl.when(ta == 0)
    def _():
        for frame in range(2):
            ahead(frame).wait_recv()
            middle(frames + frame, future.at[frame])

    for e in range(frames):
        for side in range(2):
            @pl.when(takes[side])
            def _():
                halo(side, e).wait_recv()

        if e < 2:
            @pl.when(ta == 1)
            def _():
                for side in range(2):
                    relay(side, e).start()

        if e == frames - 1:
            @pl.when(ta == 0)
            def _():
                for frame in range(2):
                    for side in range(2):
                        relay(side, frame).wait_recv()
                    outer(frames + frame)

        outer(e)

    per = rows // CHUNKS

    def pair(chunk):
        part = pl.ds(chunk * per, per)
        return pltpu.make_async_remote_copy(
            src_ref=give.at[part],
            dst_ref=got.at[part],
            send_sem=pair_send.at[chunk],
            recv_sem=pair_recv.at[chunk],
            device_id=(ha, mate),
            device_id_type=MESH,
        )

    def spread(h, slot):
        return pltpu.make_async_remote_copy(
            src_ref=out.at[h],
            dst_ref=landed.at[slot],
            send_sem=spread_send.at[h],
            recv_sem=spread_recv.at[slot],
            device_id=(h, ta),
            device_id_type=MESH,
        )

    for chunk in range(CHUNKS):
        def pick(h, _):
            give[h] = acc[pl.ds((cores * h + mate) * share, tall)]
            return 0

        lax.fori_loop(chunk * per, (chunk + 1) * per, pick, 0)
        pair(chunk).start()

    for chunk in range(CHUNKS):
        pair(chunk).wait_recv()

    def scatter(s, _):
        h = lax.rem(ha + s, rows)
        mine = acc[pl.ds((cores * h + ta) * share, tall)] + got[h]
        out[h] = mine.astype(out.dtype)
        spread(h, ha).start()
        return 0

    lax.fori_loop(1, rows, scatter, 0)

    def finish(t, _):
        summed = (
            partial[t, LEAD + 1 : LEAD + 1 + breadth, :channels]
            + partial[t, LEAD : LEAD + breadth, channels : 2 * channels]
            + partial[t, LEAD - 1 : LEAD - 1 + breadth, 2 * channels :]
        )
        v = feat[t].astype(jnp.float32)
        s = 1.0 / (1.0 + jnp.exp(-v))
        slope = s * (1.0 + v * (1.0 - s))
        grad_features[t] = (cot[t].astype(jnp.float32) + slope * summed).astype(grad_features.dtype)
        return 0

    lax.fori_loop(0, frames, finish, 0)

    total = acc[pl.ds((cores * ha + ta) * share, tall)] + got[ha]

    def collect(s, total):
        h = lax.rem(ha + rows - s, rows)
        spread(h, h).wait_recv()
        return total + landed[h].astype(jnp.float32)

    total = lax.fori_loop(1, rows, collect, total)
    grad_kernel[...] = total[:share] * factor

    def drain(s, _):
        h = lax.rem(ha + s, rows)
        spread(h, ha).wait_send()
        return 0

    lax.fori_loop(1, rows, drain, 0)
    for chunk in range(CHUNKS):
        pair(chunk).wait_send()
    for frame in range(frames):
        for side in range(2):
            @pl.when(sends[side])
            def _():
                halo(side, frame).wait_send()

    @pl.when(ta == 1)
    def _():
        for frame in range(2):
            ahead(frame).wait_send()
            for side in range(2):
                relay(side, frame).wait_send()


def body(features, cotangent, kernel):
    frames, height, breadth, channels = features.shape
    rows, cores = lax.axis_size("ha"), lax.axis_size("ta")
    taps = kernel.shape[0] * kernel.shape[1] * kernel.shape[2]
    wide = 3 * channels
    share = taps * channels // (rows * cores)
    tall = -(-share // 16) * 16
    factor = float(frames * height * breadth * rows * cores) ** (-0.5)
    vmem = pl.BlockSpec(memory_space=pltpu.VMEM)
    dma = pltpu.SemaphoreType.DMA
    grad_features, grad_kernel = pl.pallas_call(
        functools.partial(fused, rows, cores, factor),
        out_shape=(
            jax.ShapeDtypeStruct((frames, breadth, channels), jnp.bfloat16),
            jax.ShapeDtypeStruct((share, channels), jnp.float32),
        ),
        in_specs=[vmem] * 3,
        out_specs=(vmem, vmem),
        scratch_shapes=[
            pltpu.VMEM((2, frames + 2, breadth, channels), jnp.bfloat16),
            pltpu.VMEM((2, breadth, channels), jnp.bfloat16),
            pltpu.VMEM((frames, breadth, wide), jnp.bfloat16),
            pltpu.VMEM((breadth + 2 * LEAD, channels), jnp.float32),
            pltpu.VMEM((frames, breadth + 2 * LEAD, wide), jnp.float32),
            pltpu.VMEM((taps * channels + 16, channels), jnp.float32),
            pltpu.VMEM((rows, tall, channels), jnp.float32),
            pltpu.VMEM((rows, tall, channels), jnp.float32),
            pltpu.VMEM((rows, tall, channels), jnp.bfloat16),
            pltpu.VMEM((rows, tall, channels), jnp.bfloat16),
            dma((2, frames)), dma((2, frames)), dma((2,)), dma((2,)), dma((2, 2)), dma((2, 2)),
            dma((CHUNKS,)), dma((CHUNKS,)), dma((rows,)), dma((rows,)),
        ],
        compiler_params=pltpu.CompilerParams(
            collective_id=0, has_side_effects=True, vmem_limit_bytes=48 * 1024 * 1024
        ),
        cost_estimate=pl.CostEstimate(
            flops=4 * frames * breadth * taps * channels * channels,
            bytes_accessed=6 * frames * breadth * channels + 2 * taps * channels * channels,
            transcendentals=2 * frames * breadth * channels,
        ),
    )(
        features.reshape(frames, breadth, channels),
        cotangent.reshape(frames, breadth, channels),
        kernel.reshape(9, wide, channels),
    )
    return (grad_features.reshape(features.shape), grad_kernel)


def solution(mesh):
    placed = (P("ta", "ha", None, None), P("ta", "ha", None, None), P())
    return jax.shard_map(
        body,
        mesh=mesh,
        in_specs=placed,
        out_specs=(P("ta", "ha", None, None), P(("ha", "ta"), None)),
        check_vma=False,
    )
```

```python
import functools

import jax
import jax.numpy as jnp
from jax import lax
from jax.experimental import pallas as pl
from jax.experimental.pallas import tpu as pltpu
from jax.sharding import PartitionSpec as P

MESH = pl.DeviceIdType.MESH
LEAD = 8
CHUNKS = 4


def fused(
    rows, cores, factor,
    feat_hbm, cot_hbm, kern_hbm, grad_features, grad_kernel,
    feat, cot, kern, load_sem, ext, future, acts, padded, partial, acc, give, got, out, landed,
    near_send, near_recv, far_send, far_recv, future_send, future_recv, pass_send, pass_recv,
    pair_send, pair_recv, spread_send, spread_recv,
):
    frames, breadth, channels = feat.shape
    wide = 3 * channels
    share, tall = grad_kernel.shape[0], give.shape[1]
    ha, ta = lax.axis_index("ha"), lax.axis_index("ta")
    mate = 1 - ta

    loads = [
        pltpu.make_async_copy(source, target, load_sem.at[slot])
        for slot, (source, target) in enumerate(((feat_hbm, feat), (cot_hbm, cot), (kern_hbm, kern)))
    ]
    for load in loads:
        load.start()

    barrier = pltpu.get_barrier_semaphore()

    def greet(s, _):
        pl.semaphore_signal(barrier, inc=1, device_id=(lax.rem(ha + s, rows), ta), device_id_type=MESH)
        return 0

    lax.fori_loop(1, rows, greet, 0)
    pl.semaphore_signal(barrier, inc=1, device_id=(ha, mate), device_id_type=MESH)
    pl.semaphore_wait(barrier, rows)

    odd = lax.rem(ha, 2)
    near_side, far_side = 1 - odd, odd

    def near(frame, side):
        return pltpu.make_async_remote_copy(
            src_ref=cot_hbm.at[frame],
            dst_ref=ext.at[side, frame],
            send_sem=near_send.at[frame],
            recv_sem=near_recv.at[frame],
            device_id=(ha + 1 - 2 * odd, ta),
            device_id_type=MESH,
        )

    def far(frame):
        return pltpu.make_async_remote_copy(
            src_ref=ext.at[near_side, frame],
            dst_ref=ext.at[far_side, frame],
            send_sem=far_send.at[frame],
            recv_sem=far_recv.at[frame],
            device_id=(ha + 2 - 4 * odd, ta),
            device_id_type=MESH,
        )

    def ahead(frame):
        return pltpu.make_async_remote_copy(
            src_ref=cot_hbm.at[frame],
            dst_ref=future.at[frame],
            send_sem=future_send.at[frame],
            recv_sem=future_recv.at[frame],
            device_id=(ha, mate),
            device_id_type=MESH,
        )

    def relay(side, kind, frame):
        return pltpu.make_async_remote_copy(
            src_ref=ext.at[side, frame],
            dst_ref=ext.at[side, frames + frame],
            send_sem=pass_send.at[kind, frame],
            recv_sem=pass_recv.at[kind, frame],
            device_id=(ha, mate),
            device_id_type=MESH,
        )

    first, last = ha < 2, ha >= rows - 2
    even = odd == 0
    hands_on = jnp.logical_not(jnp.logical_or(jnp.logical_and(even, last), jnp.logical_and(odd == 1, first)))
    takes = jnp.logical_not(jnp.logical_or(jnp.logical_and(even, first), jnp.logical_and(odd == 1, last)))

    for frame in range(frames):
        near(frame, far_side).start()

    @pl.when(ta == 1)
    def _():
        for frame in range(2):
            ahead(frame).start()

    @pl.when(jnp.logical_not(takes))
    def _():
        ext[far_side, :frames] = jnp.zeros((frames, breadth, channels), ext.dtype)

    edge = jnp.zeros((LEAD, channels), jnp.float32)
    padded[:LEAD] = edge
    padded[LEAD + breadth :] = edge
    acc[...] = jnp.zeros_like(acc)
    loads[0].wait()

    def activate(t, _):
        v = feat[t].astype(jnp.float32)
        active = v / (1.0 + jnp.exp(-v))
        padded[LEAD : LEAD + breadth] = active
        for k in range(3):
            acts[t, :, k * channels : (k + 1) * channels] = padded[
                LEAD - 1 + k : LEAD - 1 + k + breadth
            ].astype(jnp.bfloat16)
        partial[t] = jnp.zeros(partial.shape[1:], jnp.float32)
        return 0

    lax.fori_loop(0, frames, activate, 0)

    nt = (((1,), (1,)), ((), ()))
    tn = (((0,), (0,)), ((), ()))

    def span(e):
        return max(0, e - 2), min(frames, e + 1)

    def middle(e, source):
        def step(t, _):
            i = t - e + 2
            block = source[...]
            tap = i * 3 + 1
            partial[t, LEAD : LEAD + breadth] += lax.dot_general(
                block, kern[tap], nt, preferred_element_type=jnp.float32
            )
            start = pl.multiple_of(tap * wide, wide)
            acc[pl.ds(start, wide)] += lax.dot_general(
                acts[t], block, tn, preferred_element_type=jnp.float32
            )
            return 0

        lax.fori_loop(*span(e), step, 0)

    def outer_kernel(e):
        def step(t, _):
            i = t - e + 2
            block = jnp.concatenate([ext[0, e], ext[1, e]], axis=1)
            both = lax.dot_general(acts[t], block, tn, preferred_element_type=jnp.float32)
            low = pl.multiple_of((i * 3 + 2) * wide, wide)
            high = pl.multiple_of(i * 3 * wide, wide)
            acc[pl.ds(low, wide)] += both[:, :channels]
            acc[pl.ds(high, wide)] += both[:, channels:]
            return 0

        lax.fori_loop(*span(e), step, 0)

    def outer_input(e):
        def step(t, _):
            i = t - e + 2
            block = jnp.concatenate([ext[0, e], ext[1, e]], axis=1)
            weights = jnp.concatenate([kern[i * 3 + 2], kern[i * 3]], axis=1)
            partial[t, LEAD : LEAD + breadth] += lax.dot_general(
                block, weights, nt, preferred_element_type=jnp.float32
            )
            return 0

        lax.fori_loop(*span(e), step, 0)

    def hand_on(e):
        near(e, near_side).wait_recv()

        @pl.when(hands_on)
        def _():
            far(e).start()

        if e < 2:
            @pl.when(ta == 1)
            def _():
                relay(near_side, 0, e).start()

    def arrive(e):
        @pl.when(takes)
        def _():
            far(e).wait_recv()

        if e < 2:
            @pl.when(ta == 1)
            def _():
                relay(far_side, 1, e).start()

    loads[1].wait()
    loads[2].wait()
    hand_on(0)
    middle(0, cot.at[0])
    middle(1, cot.at[1])
    hand_on(1)
    middle(2, cot.at[2])
    hand_on(2)
    arrive(0)
    outer_kernel(0)
    middle(3, cot.at[3])
    hand_on(3)
    arrive(1)
    outer_kernel(1)

    @pl.when(ta == 0)
    def _():
        for frame in range(2):
            ahead(frame).wait_recv()
            middle(frames + frame, future.at[frame])

    arrive(2)
    outer_kernel(2)

    @pl.when(ta == 0)
    def _():
        for frame in range(2):
            relay(near_side, 0, frame).wait_recv()
            relay(far_side, 1, frame).wait_recv()
            outer_kernel(frames + frame)

    arrive(3)
    outer_kernel(3)

    per = rows // CHUNKS

    def pair(chunk):
        part = pl.ds(chunk * per, per)
        return pltpu.make_async_remote_copy(
            src_ref=give.at[part],
            dst_ref=got.at[part],
            send_sem=pair_send.at[chunk],
            recv_sem=pair_recv.at[chunk],
            device_id=(ha, mate),
            device_id_type=MESH,
        )

    def spread(h, slot):
        return pltpu.make_async_remote_copy(
            src_ref=out.at[h],
            dst_ref=landed.at[slot],
            send_sem=spread_send.at[h],
            recv_sem=spread_recv.at[slot],
            device_id=(h, ta),
            device_id_type=MESH,
        )

    order = [lax.rem(ha // per + 1 + turn, CHUNKS) for turn in range(CHUNKS)]

    def pick(h, _):
        give[h] = acc[pl.ds((cores * h + mate) * share, tall)]
        return 0

    for chunk in order:
        lax.fori_loop(chunk * per, chunk * per + per, pick, 0)
        pair(chunk).start()

    def scatter(s, chunk):
        h = chunk * per + lax.rem(ha + s, per)

        @pl.when(h != ha)
        def _():
            mine = acc[pl.ds((cores * h + ta) * share, tall)] + got[h]
            out[h] = mine.astype(out.dtype)
            spread(h, ha).start()

        return chunk

    for chunk in order:
        pair(chunk).wait_recv()
        lax.fori_loop(0, per, scatter, chunk)

    for e in range(frames):
        outer_input(e)

    @pl.when(ta == 0)
    def _():
        for frame in range(2):
            outer_input(frames + frame)

    def finish(t, _):
        summed = (
            partial[t, LEAD + 1 : LEAD + 1 + breadth, :channels]
            + partial[t, LEAD : LEAD + breadth, channels : 2 * channels]
            + partial[t, LEAD - 1 : LEAD - 1 + breadth, 2 * channels :]
        )
        v = feat[t].astype(jnp.float32)
        s = 1.0 / (1.0 + jnp.exp(-v))
        slope = s * (1.0 + v * (1.0 - s))
        grad_features[t] = (cot[t].astype(jnp.float32) + slope * summed).astype(grad_features.dtype)
        return 0

    lax.fori_loop(0, frames, finish, 0)

    total = acc[pl.ds((cores * ha + ta) * share, tall)] + got[ha]

    def collect(s, total):
        h = lax.rem(ha + rows - s, rows)
        spread(h, h).wait_recv()
        return total + landed[h].astype(jnp.float32)

    total = lax.fori_loop(1, rows, collect, total)
    grad_kernel[...] = total[:share] * factor

    def drain(s, _):
        h = lax.rem(ha + s, rows)
        spread(h, ha).wait_send()
        return 0

    lax.fori_loop(1, rows, drain, 0)
    for chunk in range(CHUNKS):
        pair(chunk).wait_send()
    for frame in range(frames):
        near(frame, far_side).wait_send()

        @pl.when(hands_on)
        def _():
            far(frame).wait_send()

    @pl.when(ta == 1)
    def _():
        for frame in range(2):
            ahead(frame).wait_send()
            relay(near_side, 0, frame).wait_send()
            relay(far_side, 1, frame).wait_send()


def body(features, cotangent, kernel):
    frames, height, breadth, channels = features.shape
    rows, cores = lax.axis_size("ha"), lax.axis_size("ta")
    taps = kernel.shape[0] * kernel.shape[1] * kernel.shape[2]
    wide = 3 * channels
    share = taps * channels // (rows * cores)
    tall = -(-share // 16) * 16
    factor = float(frames * height * breadth * rows * cores) ** (-0.5)
    vmem = pl.BlockSpec(memory_space=pltpu.VMEM)
    dma = pltpu.SemaphoreType.DMA
    grad_features, grad_kernel = pl.pallas_call(
        functools.partial(fused, rows, cores, factor),
        out_shape=(
            jax.ShapeDtypeStruct((frames, breadth, channels), jnp.bfloat16),
            jax.ShapeDtypeStruct((share, channels), jnp.float32),
        ),
        in_specs=[pl.BlockSpec(memory_space=pltpu.HBM)] * 3,
        out_specs=(vmem, vmem),
        scratch_shapes=[
            pltpu.VMEM((frames, breadth, channels), jnp.bfloat16),
            pltpu.VMEM((frames, breadth, channels), jnp.bfloat16),
            pltpu.VMEM((9, wide, channels), jnp.bfloat16),
            dma((3,)),
            pltpu.VMEM((2, frames + 2, breadth, channels), jnp.bfloat16),
            pltpu.VMEM((2, breadth, channels), jnp.bfloat16),
            pltpu.VMEM((frames, breadth, wide), jnp.bfloat16),
            pltpu.VMEM((breadth + 2 * LEAD, channels), jnp.float32),
            pltpu.VMEM((frames, breadth + 2 * LEAD, wide), jnp.float32),
            pltpu.VMEM((taps * channels + 16, channels), jnp.float32),
            pltpu.VMEM((rows, tall, channels), jnp.float32),
            pltpu.VMEM((rows, tall, channels), jnp.float32),
            pltpu.VMEM((rows, tall, channels), jnp.bfloat16),
            pltpu.VMEM((rows, tall, channels), jnp.bfloat16),
            dma((frames,)), dma((frames,)), dma((frames,)), dma((frames,)), dma((2,)), dma((2,)), dma((2, 2)), dma((2, 2)),
            dma((CHUNKS,)), dma((CHUNKS,)), dma((rows,)), dma((rows,)),
        ],
        compiler_params=pltpu.CompilerParams(
            collective_id=0, has_side_effects=True, vmem_limit_bytes=48 * 1024 * 1024
        ),
        cost_estimate=pl.CostEstimate(
            flops=4 * frames * breadth * taps * channels * channels,
            bytes_accessed=6 * frames * breadth * channels + 2 * taps * channels * channels,
            transcendentals=2 * frames * breadth * channels,
        ),
    )(
        features.reshape(frames, breadth, channels),
        cotangent.reshape(frames, breadth, channels),
        kernel.reshape(9, wide, channels),
    )
    return (grad_features.reshape(features.shape), grad_kernel)


def solution(mesh):
    placed = (P("ta", "ha", None, None), P("ta", "ha", None, None), P())
    return jax.shard_map(
        body,
        mesh=mesh,
        in_specs=placed,
        out_specs=(P("ta", "ha", None, None), P(("ha", "ta"), None)),
        check_vma=False,
    )
```

```python
import functools

import jax
import jax.numpy as jnp
from jax import lax
from jax.experimental import pallas as pl
from jax.experimental.pallas import tpu as pltpu
from jax.sharding import PartitionSpec as P

MESH = pl.DeviceIdType.MESH
LEAD = 8
CHUNKS = 4
HALVES = 2


def fused(
    rows, cores, factor,
    feat_hbm, cot_hbm, kern_hbm, grad_features, grad_kernel,
    feat, cot, kern, load_sem, ext, future, acts, padded, partial, acc, give, got, out, landed,
    near_send, near_recv, far_send, far_recv, future_send, future_recv, pass_send, pass_recv,
    pair_send, pair_recv, spread_send, spread_recv,
):
    frames, breadth, channels = feat.shape
    wide = 3 * channels
    share, tall = grad_kernel.shape[0], give.shape[1]
    ha, ta = lax.axis_index("ha"), lax.axis_index("ta")
    mate = 1 - ta

    loads = [
        pltpu.make_async_copy(source, target, load_sem.at[slot])
        for slot, (source, target) in enumerate(((feat_hbm, feat), (cot_hbm, cot), (kern_hbm, kern)))
    ]
    for load in loads:
        load.start()

    barrier = pltpu.get_barrier_semaphore()

    def greet(s, _):
        pl.semaphore_signal(barrier, inc=1, device_id=(lax.rem(ha + s, rows), ta), device_id_type=MESH)
        return 0

    lax.fori_loop(1, rows, greet, 0)
    pl.semaphore_signal(barrier, inc=1, device_id=(ha, mate), device_id_type=MESH)
    pl.semaphore_wait(barrier, rows)

    odd = lax.rem(ha, 2)
    near_side, far_side = 1 - odd, odd

    def near(piece, side):
        frame, part = piece // HALVES, pl.ds(piece % HALVES * (breadth // HALVES), breadth // HALVES)
        return pltpu.make_async_remote_copy(
            src_ref=cot_hbm.at[frame, part],
            dst_ref=ext.at[side, frame, part],
            send_sem=near_send.at[piece],
            recv_sem=near_recv.at[piece],
            device_id=(ha + 1 - 2 * odd, ta),
            device_id_type=MESH,
        )

    def far(piece):
        frame, part = piece // HALVES, pl.ds(piece % HALVES * (breadth // HALVES), breadth // HALVES)
        return pltpu.make_async_remote_copy(
            src_ref=ext.at[near_side, frame, part],
            dst_ref=ext.at[far_side, frame, part],
            send_sem=far_send.at[piece],
            recv_sem=far_recv.at[piece],
            device_id=(ha + 2 - 4 * odd, ta),
            device_id_type=MESH,
        )

    def ahead(frame):
        return pltpu.make_async_remote_copy(
            src_ref=cot_hbm.at[frame],
            dst_ref=future.at[frame],
            send_sem=future_send.at[frame],
            recv_sem=future_recv.at[frame],
            device_id=(ha, mate),
            device_id_type=MESH,
        )

    def relay(side, kind, frame):
        return pltpu.make_async_remote_copy(
            src_ref=ext.at[side, frame],
            dst_ref=ext.at[side, frames + frame],
            send_sem=pass_send.at[kind, frame],
            recv_sem=pass_recv.at[kind, frame],
            device_id=(ha, mate),
            device_id_type=MESH,
        )

    first, last = ha < 2, ha >= rows - 2
    even = odd == 0
    hands_on = jnp.logical_not(jnp.logical_or(jnp.logical_and(even, last), jnp.logical_and(odd == 1, first)))
    takes = jnp.logical_not(jnp.logical_or(jnp.logical_and(even, first), jnp.logical_and(odd == 1, last)))

    for piece in range(frames * HALVES):
        near(piece, far_side).start()

    @pl.when(ta == 1)
    def _():
        for frame in range(2):
            ahead(frame).start()

    @pl.when(jnp.logical_not(takes))
    def _():
        ext[far_side, :frames] = jnp.zeros((frames, breadth, channels), ext.dtype)

    edge = jnp.zeros((LEAD, channels), jnp.float32)
    padded[:LEAD] = edge
    padded[LEAD + breadth :] = edge
    acc[...] = jnp.zeros_like(acc)

    def activate(t, _):
        v = feat[t].astype(jnp.float32)
        active = v / (1.0 + jnp.exp(-v))
        padded[LEAD : LEAD + breadth] = active
        for k in range(3):
            acts[t, :, k * channels : (k + 1) * channels] = padded[
                LEAD - 1 + k : LEAD - 1 + k + breadth
            ].astype(jnp.bfloat16)
        partial[t] = jnp.zeros(partial.shape[1:], jnp.float32)
        return 0


    nt = (((1,), (1,)), ((), ()))
    tn = (((0,), (0,)), ((), ()))

    def span(e):
        return max(0, e - 2), min(frames, e + 1)

    def middle(e, source):
        def step(t, _):
            i = t - e + 2
            block = source[...]
            tap = i * 3 + 1
            partial[t, LEAD : LEAD + breadth] += lax.dot_general(
                block, kern[tap], nt, preferred_element_type=jnp.float32
            )
            start = pl.multiple_of(tap * wide, wide)
            acc[pl.ds(start, wide)] += lax.dot_general(
                acts[t], block, tn, preferred_element_type=jnp.float32
            )
            return 0

        lax.fori_loop(*span(e), step, 0)

    def outer_kernel(e):
        def step(t, _):
            i = t - e + 2
            block = jnp.concatenate([ext[0, e], ext[1, e]], axis=1)
            both = lax.dot_general(acts[t], block, tn, preferred_element_type=jnp.float32)
            low = pl.multiple_of((i * 3 + 2) * wide, wide)
            high = pl.multiple_of(i * 3 * wide, wide)
            acc[pl.ds(low, wide)] += both[:, :channels]
            acc[pl.ds(high, wide)] += both[:, channels:]
            return 0

        lax.fori_loop(*span(e), step, 0)

    def outer_input(e):
        def step(t, _):
            i = t - e + 2
            block = jnp.concatenate([ext[0, e], ext[1, e]], axis=1)
            weights = jnp.concatenate([kern[i * 3 + 2], kern[i * 3]], axis=1)
            partial[t, LEAD : LEAD + breadth] += lax.dot_general(
                block, weights, nt, preferred_element_type=jnp.float32
            )
            return 0

        lax.fori_loop(*span(e), step, 0)

    def hand_on(e):
        near(e, near_side).wait_recv()

        @pl.when(hands_on)
        def _():
            far(e).start()

        if e % HALVES == HALVES - 1 and e // HALVES < 2:
            @pl.when(ta == 1)
            def _():
                relay(near_side, 0, e // HALVES).start()

    def arrive(e):
        @pl.when(takes)
        def _():
            for part in range(HALVES):
                far(e * HALVES + part).wait_recv()

        if e < 2:
            @pl.when(ta == 1)
            def _():
                relay(far_side, 1, e).start()

    loads[0].wait()
    hand_on(0)
    lax.fori_loop(0, 2, activate, 0)
    hand_on(1)
    lax.fori_loop(2, frames, activate, 0)
    loads[1].wait()
    loads[2].wait()
    hand_on(2)
    middle(0, cot.at[0])
    hand_on(3)
    middle(1, cot.at[1])
    hand_on(4)
    middle(2, cot.at[2])
    hand_on(5)
    arrive(0)
    outer_kernel(0)
    hand_on(6)
    middle(3, cot.at[3])
    hand_on(7)
    arrive(1)
    outer_kernel(1)

    @pl.when(ta == 0)
    def _():
        for frame in range(2):
            ahead(frame).wait_recv()
            middle(frames + frame, future.at[frame])

    arrive(2)
    outer_kernel(2)

    @pl.when(ta == 0)
    def _():
        for frame in range(2):
            relay(near_side, 0, frame).wait_recv()
            relay(far_side, 1, frame).wait_recv()
            outer_kernel(frames + frame)

    arrive(3)
    outer_kernel(3)

    per = rows // CHUNKS

    def pair(chunk):
        part = pl.ds(chunk * per, per)
        return pltpu.make_async_remote_copy(
            src_ref=give.at[part],
            dst_ref=got.at[part],
            send_sem=pair_send.at[chunk],
            recv_sem=pair_recv.at[chunk],
            device_id=(ha, mate),
            device_id_type=MESH,
        )

    def spread(h, slot):
        return pltpu.make_async_remote_copy(
            src_ref=out.at[h],
            dst_ref=landed.at[slot],
            send_sem=spread_send.at[h],
            recv_sem=spread_recv.at[slot],
            device_id=(h, ta),
            device_id_type=MESH,
        )

    order = [lax.rem(ha // per + 1 + turn, CHUNKS) for turn in range(CHUNKS)]

    def pick(h, _):
        give[h] = acc[pl.ds((cores * h + mate) * share, tall)]
        return 0

    for chunk in order:
        lax.fori_loop(chunk * per, chunk * per + per, pick, 0)
        pair(chunk).start()

    def scatter(s, chunk):
        h = chunk * per + lax.rem(ha + s, per)

        @pl.when(h != ha)
        def _():
            mine = acc[pl.ds((cores * h + ta) * share, tall)] + got[h]
            out[h] = mine.astype(out.dtype)
            spread(h, ha).start()

        return chunk

    for chunk in order:
        pair(chunk).wait_recv()
        lax.fori_loop(0, per, scatter, chunk)

    for e in range(frames):
        outer_input(e)

    @pl.when(ta == 0)
    def _():
        for frame in range(2):
            outer_input(frames + frame)

    def finish(t, _):
        summed = (
            partial[t, LEAD + 1 : LEAD + 1 + breadth, :channels]
            + partial[t, LEAD : LEAD + breadth, channels : 2 * channels]
            + partial[t, LEAD - 1 : LEAD - 1 + breadth, 2 * channels :]
        )
        v = feat[t].astype(jnp.float32)
        s = 1.0 / (1.0 + jnp.exp(-v))
        slope = s * (1.0 + v * (1.0 - s))
        grad_features[t] = (cot[t].astype(jnp.float32) + slope * summed).astype(grad_features.dtype)
        return 0

    lax.fori_loop(0, frames, finish, 0)

    total = acc[pl.ds((cores * ha + ta) * share, tall)] + got[ha]

    def collect(s, total):
        h = lax.rem(ha + rows - s, rows)
        spread(h, h).wait_recv()
        return total + landed[h].astype(jnp.float32)

    total = lax.fori_loop(1, rows, collect, total)
    grad_kernel[...] = total[:share] * factor

    def drain(s, _):
        h = lax.rem(ha + s, rows)
        spread(h, ha).wait_send()
        return 0

    lax.fori_loop(1, rows, drain, 0)
    for chunk in range(CHUNKS):
        pair(chunk).wait_send()
    for piece in range(frames * HALVES):
        near(piece, far_side).wait_send()

        @pl.when(hands_on)
        def _():
            far(piece).wait_send()

    @pl.when(ta == 1)
    def _():
        for frame in range(2):
            ahead(frame).wait_send()
            relay(near_side, 0, frame).wait_send()
            relay(far_side, 1, frame).wait_send()


def body(features, cotangent, kernel):
    frames, height, breadth, channels = features.shape
    rows, cores = lax.axis_size("ha"), lax.axis_size("ta")
    taps = kernel.shape[0] * kernel.shape[1] * kernel.shape[2]
    wide = 3 * channels
    share = taps * channels // (rows * cores)
    tall = -(-share // 16) * 16
    factor = float(frames * height * breadth * rows * cores) ** (-0.5)
    vmem = pl.BlockSpec(memory_space=pltpu.VMEM)
    dma = pltpu.SemaphoreType.DMA
    grad_features, grad_kernel = pl.pallas_call(
        functools.partial(fused, rows, cores, factor),
        out_shape=(
            pltpu.VMEM((frames, breadth, channels), jnp.bfloat16),
            pltpu.VMEM((share, channels), jnp.float32),
        ),
        in_specs=[pl.BlockSpec(memory_space=pltpu.HBM)] * 3,
        out_specs=(vmem, vmem),
        scratch_shapes=[
            pltpu.VMEM((frames, breadth, channels), jnp.bfloat16),
            pltpu.VMEM((frames, breadth, channels), jnp.bfloat16),
            pltpu.VMEM((9, wide, channels), jnp.bfloat16),
            dma((3,)),
            pltpu.VMEM((2, frames + 2, breadth, channels), jnp.bfloat16),
            pltpu.VMEM((2, breadth, channels), jnp.bfloat16),
            pltpu.VMEM((frames, breadth, wide), jnp.bfloat16),
            pltpu.VMEM((breadth + 2 * LEAD, channels), jnp.float32),
            pltpu.VMEM((frames, breadth + 2 * LEAD, wide), jnp.float32),
            pltpu.VMEM((taps * channels + 16, channels), jnp.float32),
            pltpu.VMEM((rows, tall, channels), jnp.float32),
            pltpu.VMEM((rows, tall, channels), jnp.float32),
            pltpu.VMEM((rows, tall, channels), jnp.bfloat16),
            pltpu.VMEM((rows, tall, channels), jnp.bfloat16),
            dma((frames * HALVES,)), dma((frames * HALVES,)), dma((frames * HALVES,)), dma((frames * HALVES,)), dma((2,)), dma((2,)), dma((2, 2)), dma((2, 2)),
            dma((CHUNKS,)), dma((CHUNKS,)), dma((rows,)), dma((rows,)),
        ],
        compiler_params=pltpu.CompilerParams(
            collective_id=0, has_side_effects=True, vmem_limit_bytes=63 * 1024 * 1024
        ),
        cost_estimate=pl.CostEstimate(
            flops=4 * frames * breadth * taps * channels * channels,
            bytes_accessed=6 * frames * breadth * channels + 2 * taps * channels * channels,
            transcendentals=2 * frames * breadth * channels,
        ),
    )(
        features.reshape(frames, breadth, channels),
        cotangent.reshape(frames, breadth, channels),
        kernel.reshape(9, wide, channels),
    )
    return (grad_features.reshape(features.shape), grad_kernel)


def solution(mesh):
    placed = (P("ta", "ha", None, None), P("ta", "ha", None, None), P())
    return jax.shard_map(
        body,
        mesh=mesh,
        in_specs=placed,
        out_specs=(P("ta", "ha", None, None), P(("ha", "ta"), None)),
        check_vma=False,
    )
```

```python
import functools

import jax
import jax.numpy as jnp
from jax import lax
from jax.experimental import pallas as pl
from jax.experimental.pallas import tpu as pltpu
from jax.sharding import PartitionSpec as P

MESH = pl.DeviceIdType.MESH
LEAD = 8
CHUNKS = 4
HALVES = 2


def fused(
    rows, cores, factor,
    feat_hbm, cot_hbm, kern_hbm, grad_features, grad_kernel,
    feat, cot, kern, load_sem, ext, future, acts, padded, partial, acc, give, got, out, landed,
    near_send, near_recv, far_send, far_recv, future_send, future_recv, pass_send, pass_recv,
    pair_send, pair_recv, spread_send, spread_recv,
):
    frames, breadth, channels = feat.shape
    wide = 3 * channels
    share, tall = grad_kernel.shape[0], give.shape[1]
    ha, ta = lax.axis_index("ha"), lax.axis_index("ta")
    mate = 1 - ta

    loads = [
        pltpu.make_async_copy(source, target, load_sem.at[slot])
        for slot, (source, target) in enumerate(((feat_hbm, feat), (cot_hbm, cot), (kern_hbm, kern)))
    ]
    for load in loads:
        load.start()

    barrier = pltpu.get_barrier_semaphore()

    def greet(s, _):
        pl.semaphore_signal(barrier, inc=1, device_id=(lax.rem(ha + s, rows), ta), device_id_type=MESH)
        return 0

    lax.fori_loop(1, rows, greet, 0)
    pl.semaphore_signal(barrier, inc=1, device_id=(ha, mate), device_id_type=MESH)
    pl.semaphore_wait(barrier, rows)

    odd = lax.rem(ha, 2)
    near_side, far_side = 1 - odd, odd

    def near(piece, side):
        frame, part = piece // HALVES, pl.ds(piece % HALVES * (breadth // HALVES), breadth // HALVES)
        return pltpu.make_async_remote_copy(
            src_ref=cot_hbm.at[frame, part],
            dst_ref=ext.at[side, frame, part],
            send_sem=near_send.at[piece],
            recv_sem=near_recv.at[piece],
            device_id=(ha + 1 - 2 * odd, ta),
            device_id_type=MESH,
        )

    def far(piece):
        frame, part = piece // HALVES, pl.ds(piece % HALVES * (breadth // HALVES), breadth // HALVES)
        return pltpu.make_async_remote_copy(
            src_ref=ext.at[near_side, frame, part],
            dst_ref=ext.at[far_side, frame, part],
            send_sem=far_send.at[piece],
            recv_sem=far_recv.at[piece],
            device_id=(ha + 2 - 4 * odd, ta),
            device_id_type=MESH,
        )

    def ahead(frame):
        return pltpu.make_async_remote_copy(
            src_ref=cot_hbm.at[frame],
            dst_ref=future.at[frame],
            send_sem=future_send.at[frame],
            recv_sem=future_recv.at[frame],
            device_id=(ha, mate),
            device_id_type=MESH,
        )

    def relay(side, kind, frame):
        return pltpu.make_async_remote_copy(
            src_ref=ext.at[side, frame],
            dst_ref=ext.at[side, frames + frame],
            send_sem=pass_send.at[kind, frame],
            recv_sem=pass_recv.at[kind, frame],
            device_id=(ha, mate),
            device_id_type=MESH,
        )

    first, last = ha < 2, ha >= rows - 2
    even = odd == 0
    hands_on = jnp.logical_not(jnp.logical_or(jnp.logical_and(even, last), jnp.logical_and(odd == 1, first)))
    takes = jnp.logical_not(jnp.logical_or(jnp.logical_and(even, first), jnp.logical_and(odd == 1, last)))

    for piece in range(frames * HALVES):
        near(piece, far_side).start()

    @pl.when(ta == 1)
    def _():
        for frame in range(2):
            ahead(frame).start()

    @pl.when(jnp.logical_not(takes))
    def _():
        ext[far_side, :frames] = jnp.zeros((frames, breadth, channels), ext.dtype)

    edge = jnp.zeros((LEAD, channels), jnp.float32)
    padded[:LEAD] = edge
    padded[LEAD + breadth :] = edge
    acc[...] = jnp.zeros_like(acc)

    def activate(t, _):
        v = feat[t].astype(jnp.float32)
        active = v / (1.0 + jnp.exp(-v))
        padded[LEAD : LEAD + breadth] = active
        for k in range(3):
            acts[t, :, k * channels : (k + 1) * channels] = padded[
                LEAD - 1 + k : LEAD - 1 + k + breadth
            ].astype(jnp.bfloat16)
        partial[t] = jnp.zeros(partial.shape[1:], jnp.float32)
        return 0


    nt = (((1,), (1,)), ((), ()))
    tn = (((0,), (0,)), ((), ()))

    def span(e):
        return max(0, e - 2), min(frames, e + 1)

    def middle(e, source):
        def step(t, _):
            i = t - e + 2
            block = source[...]
            tap = i * 3 + 1
            partial[t, LEAD : LEAD + breadth] += lax.dot_general(
                block, kern[tap], nt, preferred_element_type=jnp.float32
            )
            start = pl.multiple_of(tap * wide, wide)
            acc[pl.ds(start, wide)] += lax.dot_general(
                acts[t], block, tn, preferred_element_type=jnp.float32
            )
            return 0

        lax.fori_loop(*span(e), step, 0)

    def outer_kernel(e):
        def step(t, _):
            i = t - e + 2
            block = jnp.concatenate([ext[0, e], ext[1, e]], axis=1)
            both = lax.dot_general(acts[t], block, tn, preferred_element_type=jnp.float32)
            low = pl.multiple_of((i * 3 + 2) * wide, wide)
            high = pl.multiple_of(i * 3 * wide, wide)
            acc[pl.ds(low, wide)] += both[:, :channels]
            acc[pl.ds(high, wide)] += both[:, channels:]
            return 0

        lax.fori_loop(*span(e), step, 0)

    def outer_input(e):
        def step(t, _):
            i = t - e + 2
            block = jnp.concatenate([ext[0, e], ext[1, e]], axis=1)
            weights = jnp.concatenate([kern[i * 3 + 2], kern[i * 3]], axis=1)
            partial[t, LEAD : LEAD + breadth] += lax.dot_general(
                block, weights, nt, preferred_element_type=jnp.float32
            )
            return 0

        lax.fori_loop(*span(e), step, 0)

    def hand_on(e):
        near(e, near_side).wait_recv()

        @pl.when(hands_on)
        def _():
            far(e).start()

        if e % HALVES == HALVES - 1 and e // HALVES < 2:
            @pl.when(ta == 1)
            def _():
                relay(near_side, 0, e // HALVES).start()

    def arrive(e):
        @pl.when(takes)
        def _():
            for part in range(HALVES):
                far(e * HALVES + part).wait_recv()

        if e < 2:
            @pl.when(ta == 1)
            def _():
                relay(far_side, 1, e).start()

    loads[0].wait()
    hand_on(0)
    lax.fori_loop(0, 2, activate, 0)
    hand_on(1)
    lax.fori_loop(2, frames, activate, 0)
    loads[1].wait()
    loads[2].wait()
    hand_on(2)
    middle(0, cot.at[0])
    hand_on(3)
    middle(1, cot.at[1])
    hand_on(4)
    middle(2, cot.at[2])
    hand_on(5)
    arrive(0)
    outer_kernel(0)
    hand_on(6)
    middle(3, cot.at[3])
    hand_on(7)
    arrive(1)
    outer_kernel(1)

    @pl.when(ta == 0)
    def _():
        for frame in range(2):
            ahead(frame).wait_recv()
            middle(frames + frame, future.at[frame])

    arrive(2)
    outer_kernel(2)

    @pl.when(ta == 0)
    def _():
        for frame in range(2):
            relay(near_side, 0, frame).wait_recv()
            relay(far_side, 1, frame).wait_recv()
            outer_kernel(frames + frame)

    arrive(3)
    outer_kernel(3)

    per = rows // CHUNKS

    def pair(chunk):
        part = pl.ds(chunk * per, per)
        return pltpu.make_async_remote_copy(
            src_ref=give.at[part],
            dst_ref=got.at[part],
            send_sem=pair_send.at[chunk],
            recv_sem=pair_recv.at[chunk],
            device_id=(ha, mate),
            device_id_type=MESH,
        )

    def spread(h, slot):
        return pltpu.make_async_remote_copy(
            src_ref=out.at[h],
            dst_ref=landed.at[slot],
            send_sem=spread_send.at[h],
            recv_sem=spread_recv.at[slot],
            device_id=(h, ta),
            device_id_type=MESH,
        )

    order = [lax.rem(ha // per + 1 + turn, CHUNKS) for turn in range(CHUNKS)]

    def pick(h, _):
        give[h] = acc[pl.ds((cores * h + mate) * share, tall)].astype(give.dtype)
        return 0

    for chunk in order:
        lax.fori_loop(chunk * per, chunk * per + per, pick, 0)
        pair(chunk).start()

    def scatter(s, chunk):
        h = chunk * per + lax.rem(ha + s, per)

        @pl.when(h != ha)
        def _():
            mine = acc[pl.ds((cores * h + ta) * share, tall)] + got[h].astype(jnp.float32)
            out[h] = mine.astype(out.dtype)
            spread(h, ha).start()

        return chunk

    for chunk in order:
        pair(chunk).wait_recv()
        lax.fori_loop(0, per, scatter, chunk)

    for e in range(frames):
        outer_input(e)

    @pl.when(ta == 0)
    def _():
        for frame in range(2):
            outer_input(frames + frame)

    def finish(t, _):
        summed = (
            partial[t, LEAD + 1 : LEAD + 1 + breadth, :channels]
            + partial[t, LEAD : LEAD + breadth, channels : 2 * channels]
            + partial[t, LEAD - 1 : LEAD - 1 + breadth, 2 * channels :]
        )
        v = feat[t].astype(jnp.float32)
        s = 1.0 / (1.0 + jnp.exp(-v))
        slope = s * (1.0 + v * (1.0 - s))
        grad_features[t] = (cot[t].astype(jnp.float32) + slope * summed).astype(grad_features.dtype)
        return 0

    lax.fori_loop(0, frames, finish, 0)

    total = acc[pl.ds((cores * ha + ta) * share, tall)] + got[ha].astype(jnp.float32)

    def collect(s, total):
        h = lax.rem(ha + rows - s, rows)
        spread(h, h).wait_recv()
        return total + landed[h].astype(jnp.float32)

    total = lax.fori_loop(1, rows, collect, total)
    grad_kernel[...] = total[:share] * factor

    def drain(s, _):
        h = lax.rem(ha + s, rows)
        spread(h, ha).wait_send()
        return 0

    lax.fori_loop(1, rows, drain, 0)
    for chunk in range(CHUNKS):
        pair(chunk).wait_send()
    for piece in range(frames * HALVES):
        near(piece, far_side).wait_send()

        @pl.when(hands_on)
        def _():
            far(piece).wait_send()

    @pl.when(ta == 1)
    def _():
        for frame in range(2):
            ahead(frame).wait_send()
            relay(near_side, 0, frame).wait_send()
            relay(far_side, 1, frame).wait_send()


def body(features, cotangent, kernel):
    frames, height, breadth, channels = features.shape
    rows, cores = lax.axis_size("ha"), lax.axis_size("ta")
    taps = kernel.shape[0] * kernel.shape[1] * kernel.shape[2]
    wide = 3 * channels
    share = taps * channels // (rows * cores)
    tall = -(-share // 16) * 16
    factor = float(frames * height * breadth * rows * cores) ** (-0.5)
    vmem = pl.BlockSpec(memory_space=pltpu.VMEM)
    dma = pltpu.SemaphoreType.DMA
    grad_features, grad_kernel = pl.pallas_call(
        functools.partial(fused, rows, cores, factor),
        out_shape=(
            pltpu.VMEM((frames, breadth, channels), jnp.bfloat16),
            pltpu.VMEM((share, channels), jnp.float32),
        ),
        in_specs=[pl.BlockSpec(memory_space=pltpu.HBM)] * 3,
        out_specs=(vmem, vmem),
        scratch_shapes=[
            pltpu.VMEM((frames, breadth, channels), jnp.bfloat16),
            pltpu.VMEM((frames, breadth, channels), jnp.bfloat16),
            pltpu.VMEM((9, wide, channels), jnp.bfloat16),
            dma((3,)),
            pltpu.VMEM((2, frames + 2, breadth, channels), jnp.bfloat16),
            pltpu.VMEM((2, breadth, channels), jnp.bfloat16),
            pltpu.VMEM((frames, breadth, wide), jnp.bfloat16),
            pltpu.VMEM((breadth + 2 * LEAD, channels), jnp.float32),
            pltpu.VMEM((frames, breadth + 2 * LEAD, wide), jnp.float32),
            pltpu.VMEM((taps * channels + 16, channels), jnp.float32),
            pltpu.VMEM((rows, tall, channels), jnp.bfloat16),
            pltpu.VMEM((rows, tall, channels), jnp.bfloat16),
            pltpu.VMEM((rows, tall, channels), jnp.bfloat16),
            pltpu.VMEM((rows, tall, channels), jnp.bfloat16),
            dma((frames * HALVES,)), dma((frames * HALVES,)), dma((frames * HALVES,)), dma((frames * HALVES,)), dma((2,)), dma((2,)), dma((2, 2)), dma((2, 2)),
            dma((CHUNKS,)), dma((CHUNKS,)), dma((rows,)), dma((rows,)),
        ],
        compiler_params=pltpu.CompilerParams(
            collective_id=0, has_side_effects=True, vmem_limit_bytes=63 * 1024 * 1024
        ),
        cost_estimate=pl.CostEstimate(
            flops=4 * frames * breadth * taps * channels * channels,
            bytes_accessed=6 * frames * breadth * channels + 2 * taps * channels * channels,
            transcendentals=2 * frames * breadth * channels,
        ),
    )(
        features.reshape(frames, breadth, channels),
        cotangent.reshape(frames, breadth, channels),
        kernel.reshape(9, wide, channels),
    )
    return (grad_features.reshape(features.shape), grad_kernel)


def solution(mesh):
    placed = (P("ta", "ha", None, None), P("ta", "ha", None, None), P())
    return jax.shard_map(
        body,
        mesh=mesh,
        in_specs=placed,
        out_specs=(P("ta", "ha", None, None), P(("ha", "ta"), None)),
        check_vma=False,
    )
```
